256 devices in a mesh: rep: 64 (over y, z_lo, x, core), fsdp: 4 (over z_hi).
Axes of the slice: x: 4, y: 4, z: 8 (z_hi: 4, z_lo: 2; z = z_hi * 2 + z_lo), core: 2. Of those that a mesh axis runs over, the one named last changes fastest.
Arguments:
- tokens: bfloat16 [64, 960, 8192], P('rep', 'fsdp'), may hold values from -6 to 6
- key_proj: bfloat16 [64, 8192, 512], P('rep', 'fsdp'), may hold values from -0.0625 to 0.0625
- cotangent: bfloat16 [64, 960, 512], P('rep', 'fsdp'), may hold values from -0.59765625 to 0.59765625
- codes: int32 [64, 131072], P('rep', 'fsdp'), may hold values from -127 to 127
- block_scales: float32 [64, 1024], P('rep', 'fsdp'), may hold values from 0.002 to 0.02
- outer_params: float32 [131072], P('fsdp'), may hold values from -6 to 6
- outer_moment: float32 [131072], P('fsdp'), may hold values from -3 to 3
Outputs:
- grad_proj: bfloat16 [64, 8192, 512], P('rep', 'fsdp')
- input_grad: bfloat16 [64, 960, 8192], P('rep', 'fsdp')
- new_params: float32 [131072], P('fsdp')
- new_moment: float32 [131072], P('fsdp')
The draws below stay inside these ranges and needn't reach their ends.
All inputs are finite; a program needn't handle non-finite values.
Results may differ from the reference program's by a relative error of at most 0.013.
Values may be sent and summed in bfloat16 or wider, within the bound.
A program may use at most 128 MiB of HBM per device.

```python
import math
import jax
import jax.numpy as jnp
from jax import lax

D = 8192
KV = 512
TOK_DEV = 240
BLOCK = 128
REPS = 64
TOK_REP = 960
FRAG = 131072
NBLOCKS = 1024
N_FSDP = 4


def set_ends(values, rng, low, largest):
    extent = values.shape
    spot = [jax.random.randint(jax.random.fold_in(rng, axis), (), 0, extent[axis]) for axis in range(len(extent))]
    values = values.at[tuple(spot)].set(low)
    longest = extent.index(max(extent))
    spot[longest] = (spot[longest] + 1) % extent[longest]
    return values.at[tuple(spot)].set(largest)


def levels(key, shape, shards, low, high):
    def one(dim, shards_of):
        draws = jax.random.uniform(jax.random.fold_in(jax.random.fold_in(key, 6), dim), (shards_of,), jnp.float32, low / len(shards), high / len(shards))
        return jnp.repeat(jnp.exp(draws), shape[dim] // shards_of).reshape((-1,) + (1,) * (len(shape) - dim - 1))

    loudness = one(*shards[0])
    for cut in shards[1:]:
        loudness = loudness * one(*cut)
    return loudness


def gaussian(own_key, dims, deviation, most, cuts=(), held_as=jnp.bfloat16):
    entries = jax.random.normal(own_key, dims, jnp.float32) * deviation
    if len(cuts) > 0:
        entries = levels(own_key, dims, cuts, -0.22, 0.18) * entries
    return jnp.clip(entries, min=-most, max=most).astype(held_as)


def setup_inputs(seed: int = 0) -> dict:
    splits = jax.random.split(jax.random.key(seed), 8)
    return {
        "tokens": gaussian(splits[0], (REPS, TOK_REP, D), 1.0, 6.0, ((0, 64), (1, 4))),
        "key_proj": gaussian(splits[1], (REPS, D, KV), D ** -0.5, 0.0625, ((0, 64), (1, 4))),
        "cotangent": gaussian(splits[2], (REPS, TOK_REP, KV), 0.1, 0.59765625, ((0, 64), (1, 4))),
        "codes": set_ends(jax.random.randint(splits[3], (REPS, FRAG), -127, 128), jax.random.fold_in(splits[3], 1), -127, 127).astype(jnp.int32),
        "block_scales": jnp.clip(jnp.exp(math.log(0.02) - 2.30258502 * jax.random.uniform(splits[4], (REPS, NBLOCKS), jnp.float32) ** levels(splits[4], (REPS, NBLOCKS), ((0, 64), (1, 4)), -0.2, 0.2)), 0.002, 0.02),
        "outer_params": gaussian(splits[5], (FRAG,), 1.0, 6.0, ((0, 4),), jnp.float32),
        "outer_moment": gaussian(splits[6], (FRAG,), 0.5, 3.0, ((0, 4),), jnp.float32),
    }


outer_rate = 0.7
outer_momentum = 0.9


def replica_step(operands):
    inputs, weights, upstream = operands
    input_grads = lax.dot_general(upstream, weights, (((1,), (1,)), ((), ())), preferred_element_type=jnp.float32).astype(jnp.bfloat16)
    grad_total = jnp.zeros((inputs.shape[1], upstream.shape[1]), jnp.float32)
    for group in range(N_FSDP):
        token_part = inputs[group * TOK_DEV:(group + 1) * TOK_DEV]
        upstream_part = upstream[group * TOK_DEV:(group + 1) * TOK_DEV]
        partial_grad = jnp.dot(token_part.T, upstream_part, preferred_element_type=jnp.float32).astype(jnp.bfloat16)
        grad_total = grad_total + partial_grad.astype(jnp.float32)
    return grad_total.astype(jnp.bfloat16), input_grads


def reference(tokens, key_proj, cotangent, codes, block_scales, outer_params, outer_moment):
    grad_proj, input_grad = lax.map(replica_step, (tokens, key_proj, cotangent))
    dequant = codes.astype(jnp.float32).reshape(REPS, NBLOCKS, BLOCK) * block_scales[:, :, None]
    total_sum = jnp.sum(dequant, axis=0).reshape(FRAG)
    outer_delta = total_sum / REPS
    new_moment = outer_momentum * outer_moment + outer_delta
    new_params = outer_params - outer_rate * (outer_delta + outer_momentum * new_moment)
    return grad_proj, input_grad, new_params, new_moment
```

```python
import functools

import jax
import jax.numpy as jnp
from jax import lax
from jax.experimental import pallas as pl
from jax.experimental.pallas import tpu as pltpu
from jax.sharding import PartitionSpec as P

BLOCK = 128
TOK = 240
KV = 512
COLS = 2048
NF = 4
OUTER_RATE = 0.7
OUTER_MOMENTUM = 0.9

WIDTH = 512
CHUNKS = COLS // WIDTH
UPPER = 128
ROWS = 256
GA = 8
GB = 8
RA = ROWS // GA
RB = RA // GB

MESH = pl.DeviceIdType.MESH


def kernel(
    tok_hbm, kp_hbm, cot_hbm, codes_hbm, scales_hbm, params_hbm, moment_hbm,
    gp_out, ig_out, np_out, nm_out,
    tok, kp, cot, ig, gp, codes, scales, params, moment,
    deq, part_a, mine_b, part_b, sum_b, full_b, sum_a, full_a,
    load_sem, store_sem,
    c_send, c_recv, f_send, f_recv,
    t_send, t_recv, i_send, i_recv,
    a_send, a_recv, b_send, b_recv, gb_send, gb_recv, ga_send, ga_recv,
):
    rep = lax.axis_index("rep")
    me = lax.axis_index("fsdp")
    a_id = lax.rem(rep, GA)
    b_id = lax.div(rep, GA)

    def peer(d):
        return lax.rem(me + d, NF)

    def fs_dev(d):
        return (rep, peer(d))

    def a_peer(k):
        return lax.rem(a_id + k, GA)

    def b_peer(k):
        return lax.rem(b_id + k, GB)

    def a_dev(k):
        return (b_id * GA + a_peer(k), me)

    def b_dev(k):
        return (b_peer(k) * GA + a_id, me)

    def remote(src, dst, send, recv, dev):
        return pltpu.make_async_remote_copy(
            src_ref=src, dst_ref=dst, send_sem=send, recv_sem=recv,
            device_id=dev, device_id_type=MESH,
        )

    barrier = pltpu.get_barrier_semaphore()
    devs = [fs_dev(d) for d in (2, 1, 3)]
    devs += [b_dev(k) for k in range(1, GB)] + [a_dev(k) for k in range(1, GA)]
    for dev in devs:
        pl.semaphore_signal(barrier, inc=1, device_id=dev, device_id_type=MESH)

    loads = [
        pltpu.make_async_copy(cot_hbm, cot.at[me], load_sem.at[0]),
        pltpu.make_async_copy(kp_hbm, kp, load_sem.at[1]),
        pltpu.make_async_copy(codes_hbm, codes, load_sem.at[2]),
        pltpu.make_async_copy(scales_hbm, scales, load_sem.at[3]),
        pltpu.make_async_copy(params_hbm, params, load_sem.at[4]),
        pltpu.make_async_copy(moment_hbm, moment, load_sem.at[5]),
        pltpu.make_async_copy(
            tok_hbm.at[:, pl.ds(pl.multiple_of(me * COLS, COLS), COLS)], tok.at[me], load_sem.at[6]
        ),
    ]
    for load in loads:
        load.start()

    pl.semaphore_wait(barrier, len(devs))

    c_copies = [
        remote(cot_hbm, cot.at[me], c_send.at[k], c_recv.at[k], fs_dev(d))
        for k, d in enumerate((1, 3))
    ]
    for copy in c_copies:
        copy.start()

    def token_copy(k, d, c):
        start = pl.multiple_of(peer(d) * COLS + c * WIDTH, WIDTH)
        return remote(
            tok_hbm.at[:, pl.ds(start, WIDTH)],
            tok.at[me, :, pl.ds(c * WIDTH, WIDTH)],
            t_send.at[k, c], t_recv.at[k, c], fs_dev(d),
        )

    t_copies = [[token_copy(k, d, c) for k, d in enumerate((2, 1, 3))] for c in range(CHUNKS)]
    for copy in t_copies[0]:
        copy.start()

    loads[2].wait()
    loads[3].wait()
    spread = jnp.transpose(jnp.broadcast_to(scales[...], (BLOCK, ROWS)))
    deq[...] = codes[...].astype(jnp.float32) * spread
    a_copies = []
    for k in range(1, GA):
        rows = pl.ds(pl.multiple_of(a_peer(k) * RA, RA), RA)
        copy = remote(deq.at[rows], part_a.at[k - 1], a_send.at[k - 1], a_recv.at[k - 1], a_dev(k))
        copy.start()
        a_copies.append(copy)

    f_copies = []
    for k, (origin, target, lo, n) in enumerate(((3, 1, 0, UPPER), (1, 3, UPPER, TOK - UPPER))):
        c_copies[k].wait_recv()
        part = cot.at[peer(origin), pl.ds(lo, n)]
        copy = remote(part, part, f_send.at[k], f_recv.at[k], fs_dev(target))
        copy.start()
        f_copies.append(copy)

    for c in range(1, CHUNKS):
        for copy in t_copies[c]:
            copy.start()

    loads[0].wait()
    loads[1].wait()

    def product(d, slot, c):
        cols = pl.ds(c * WIDTH, WIDTH)
        ig[slot, :, cols] = lax.dot_general(
            cot[peer(d)], kp[cols, :], (((1,), (1,)), ((), ())),
            preferred_element_type=jnp.float32,
        ).astype(jnp.bfloat16)

    i_copies = []

    def send_products(d, slot):
        for c in range(CHUNKS):
            product(d, slot, c)
            start = pl.multiple_of(me * COLS + c * WIDTH, WIDTH)
            copy = remote(
                ig.at[slot, :, pl.ds(c * WIDTH, WIDTH)],
                ig_out.at[:, pl.ds(start, WIDTH)],
                i_send.at[slot, c], i_recv.at[slot, c], fs_dev(d),
            )
            copy.start()
            i_copies.append(copy)

    send_products(1, 1)
    send_products(3, 2)

    for copy in a_copies:
        copy.wait_recv()
    total = deq[pl.ds(pl.multiple_of(a_id * RA, RA), RA)]
    for k in range(GA - 1):
        total = total + part_a[k]
    for b in range(GB):
        mine_b[b] = total[b * RB:(b + 1) * RB]
    b_copies = []
    for k in range(1, GB):
        copy = remote(mine_b.at[b_peer(k)], part_b.at[k - 1], b_send.at[k - 1], b_recv.at[k - 1], b_dev(k))
        copy.start()
        b_copies.append(copy)

    for copy in f_copies:
        copy.wait_recv()
    send_products(2, 0)

    for copy in b_copies:
        copy.wait_recv()
    total = mine_b[b_id]
    for k in range(GB - 1):
        total = total + part_b[k]
    sum_b[...] = total
    full_b[b_id] = total
    gb_copies = []
    for k in range(1, GB):
        copy = remote(sum_b, full_b.at[b_id], gb_send.at[k - 1], gb_recv.at[k - 1], b_dev(k))
        copy.start()
        gb_copies.append(copy)

    stores = []
    for c in range(CHUNKS):
        product(0, 3, c)
    start = pl.multiple_of(me * COLS, COLS)
    store = pltpu.make_async_copy(ig.at[3], ig_out.at[:, pl.ds(start, COLS)], store_sem.at[0])
    store.start()
    stores.append(store)

    for copy in gb_copies:
        copy.wait_recv()
    for b in range(GB):
        sum_a[b * RB:(b + 1) * RB] = full_b[b]
    full_a[a_id] = sum_a[...]
    ga_copies = []
    for k in range(1, GA):
        copy = remote(sum_a, full_a.at[a_id], ga_send.at[k - 1], ga_recv.at[k - 1], a_dev(k))
        copy.start()
        ga_copies.append(copy)

    loads[4].wait()
    loads[5].wait()
    loads[6].wait()
    for copy in ga_copies:
        copy.wait_recv()
    delta = full_a[...].reshape(ROWS, BLOCK) / (GA * GB)
    moment_next = OUTER_MOMENTUM * moment[...] + delta
    params[...] = params[...] - OUTER_RATE * (delta + OUTER_MOMENTUM * moment_next)
    moment[...] = moment_next
    for k, (src, dst) in enumerate(((params, np_out), (moment, nm_out))):
        store = pltpu.make_async_copy(src, dst, store_sem.at[1 + k])
        store.start()
        stores.append(store)

    for c in range(CHUNKS):
        for copy in t_copies[c]:
            copy.wait_recv()
        cols = pl.ds(c * WIDTH, WIDTH)
        gp[cols, :] = lax.dot_general(
            tok[:, :, cols].reshape(NF * TOK, WIDTH), cot[...].reshape(NF * TOK, KV),
            (((0,), (0,)), ((), ())), preferred_element_type=jnp.float32,
        ).astype(jnp.bfloat16)
        store = pltpu.make_async_copy(gp.at[cols], gp_out.at[cols], store_sem.at[3 + c])
        store.start()
        stores.append(store)

    for copy in i_copies:
        copy.wait_recv()
    for store in stores:
        store.wait()
    sends = c_copies + f_copies + i_copies + a_copies + b_copies + gb_copies + ga_copies
    for row in t_copies:
        sends += row
    for copy in sends:
        copy.wait_send()


def local(tokens, key_proj, cotangent, codes, block_scales, outer_params, outer_moment):
    f32, bf16 = jnp.float32, jnp.bfloat16
    any_spec = pl.BlockSpec(memory_space=pl.ANY)
    dma = pltpu.SemaphoreType.DMA
    vmem = pltpu.VMEM
    grad_proj, input_grad, new_params, new_moment = pl.pallas_call(
        kernel,
        out_shape=(
            jax.ShapeDtypeStruct((COLS, KV), bf16),
            jax.ShapeDtypeStruct((TOK, NF * COLS), bf16),
            jax.ShapeDtypeStruct((ROWS, BLOCK), f32),
            jax.ShapeDtypeStruct((ROWS, BLOCK), f32),
        ),
        in_specs=[any_spec] * 7,
        out_specs=(any_spec,) * 4,
        scratch_shapes=[
            vmem((NF, TOK, COLS), bf16),
            vmem((COLS, KV), bf16),
            vmem((NF, TOK, KV), bf16),
            vmem((NF, TOK, COLS), bf16),
            vmem((COLS, KV), bf16),
            vmem((ROWS, BLOCK), jnp.int32),
            vmem((1, ROWS), f32),
            vmem((ROWS, BLOCK), f32),
            vmem((ROWS, BLOCK), f32),
            vmem((ROWS, BLOCK), f32),
            vmem((GA - 1, RA, BLOCK), f32),
            vmem((GB, RB, BLOCK), f32),
            vmem((GB - 1, RB, BLOCK), f32),
            vmem((RB, BLOCK), f32),
            vmem((GB, RB, BLOCK), f32),
            vmem((RA, BLOCK), f32),
            vmem((GA, RA, BLOCK), f32),
            dma((7,)),
            dma((3 + CHUNKS,)),
            dma((2,)), dma((2,)), dma((2,)), dma((2,)),
            dma((3, CHUNKS)), dma((3, CHUNKS)), dma((3, CHUNKS)), dma((3, CHUNKS)),
            dma((GA - 1,)), dma((GA - 1,)), dma((GB - 1,)), dma((GB - 1,)),
            dma((GB - 1,)), dma((GB - 1,)), dma((GA - 1,)), dma((GA - 1,)),
        ],
        compiler_params=pltpu.CompilerParams(
            collective_id=0, has_side_effects=True, vmem_limit_bytes=56 * 1024 * 1024
        ),
        name="step",
    )(
        tokens[0], key_proj[0], cotangent[0], codes.reshape(ROWS, BLOCK), block_scales,
        outer_params.reshape(ROWS, BLOCK), outer_moment.reshape(ROWS, BLOCK),
    )
    return grad_proj[None], input_grad[None], new_params.reshape(-1), new_moment.reshape(-1)


def solution(mesh):
    return jax.shard_map(
        local,
        mesh=mesh,
        in_specs=(
            P("rep", "fsdp", None),
            P("rep", "fsdp", None),
            P("rep", "fsdp", None),
            P("rep", "fsdp"),
            P("rep", "fsdp"),
            P("fsdp"),
            P("fsdp"),
        ),
        out_specs=(P("rep", "fsdp", None), P("rep", "fsdp", None), P("fsdp"), P("fsdp")),
        check_vma=False,
    )
```

```python
import functools

import jax
import jax.numpy as jnp
from jax import lax
from jax.experimental import pallas as pl
from jax.experimental.pallas import tpu as pltpu
from jax.sharding import PartitionSpec as P

BLOCK = 128
TOK = 240
KV = 512
COLS = 2048
NF = 4
OUTER_RATE = 0.7
OUTER_MOMENTUM = 0.9

WIDTH = 256
CHUNKS = COLS // WIDTH
T_CUTS = ((0, 256), (256, 256), (512, 256), (768, 1280))
I_CUTS = ((0, 2048),)
UPPER = 128
ROWS = 256
GA = 8
GB = 8
RA = ROWS // GA
RB = RA // GB

ORDER = (2, 1, 3)

MESH = pl.DeviceIdType.MESH


def kernel(
    tok_hbm, kp_hbm, cot_hbm, codes_hbm, scales_hbm, params_hbm, moment_hbm,
    gp_out, ig_out, np_out, nm_out,
    tok, kp, cot, ig, codes, scales, params, moment,
    deq, part_a, mine_b, part_b, sum_b, full_b, sum_a, full_a,
    load_sem,
    c_send, c_recv, f_send, f_recv,
    t_send, t_recv, i_send, i_recv,
    a_send, a_recv, b_send, b_recv, gb_send, gb_recv, ga_send, ga_recv,
):
    rep = lax.axis_index("rep")
    me = lax.axis_index("fsdp")
    a_id = lax.rem(rep, GA)
    b_id = lax.div(rep, GA)

    def peer(d):
        return lax.rem(me + d, NF)

    def fs_dev(d):
        return (rep, peer(d))

    def a_peer(k):
        return lax.rem(a_id + k, GA)

    def b_peer(k):
        return lax.rem(b_id + k, GB)

    def a_dev(k):
        return (b_id * GA + a_peer(k), me)

    def b_dev(k):
        return (b_peer(k) * GA + a_id, me)

    def remote(src, dst, send, recv, dev):
        return pltpu.make_async_remote_copy(
            src_ref=src, dst_ref=dst, send_sem=send, recv_sem=recv,
            device_id=dev, device_id_type=MESH,
        )

    barrier = pltpu.get_barrier_semaphore()
    devs = [fs_dev(d) for d in ORDER]
    devs += [b_dev(k) for k in range(1, GB)] + [a_dev(k) for k in range(1, GA)]
    for dev in devs:
        pl.semaphore_signal(barrier, inc=1, device_id=dev, device_id_type=MESH)

    loads = [
        pltpu.make_async_copy(cot_hbm, cot.at[me], load_sem.at[0]),
        pltpu.make_async_copy(kp_hbm, kp, load_sem.at[1]),
        pltpu.make_async_copy(codes_hbm, codes, load_sem.at[2]),
        pltpu.make_async_copy(scales_hbm, scales, load_sem.at[3]),
        pltpu.make_async_copy(params_hbm, params, load_sem.at[4]),
        pltpu.make_async_copy(moment_hbm, moment, load_sem.at[5]),
        pltpu.make_async_copy(
            tok_hbm.at[:, pl.ds(pl.multiple_of(me * COLS, COLS), COLS)], tok.at[me], load_sem.at[6]
        ),
    ]
    for load in loads:
        load.start()

    pl.semaphore_wait(barrier, len(devs))

    c_copies = [
        remote(cot_hbm, cot.at[me], c_send.at[k], c_recv.at[k], fs_dev(d))
        for k, d in enumerate((1, 3))
    ]

    f_copies = []
    for k, (origin, target, lo, n) in enumerate(((3, 1, 0, UPPER), (1, 3, UPPER, TOK - UPPER))):
        part = cot.at[peer(origin), pl.ds(lo, n)]
        f_copies.append(remote(part, part, f_send.at[k], f_recv.at[k], fs_dev(target)))

    def token_copy(k, d, c):
        lo, n = T_CUTS[c]
        start = pl.multiple_of(peer(d) * COLS + lo, WIDTH)
        return remote(
            tok_hbm.at[:, pl.ds(start, n)],
            tok.at[me, :, pl.ds(lo, n)],
            t_send.at[k, c], t_recv.at[k, c], fs_dev(d),
        )

    def product_copy(k, d, c):
        lo, n = I_CUTS[c]
        start = pl.multiple_of(me * COLS + lo, WIDTH)
        return remote(
            ig.at[k, :, pl.ds(lo, n)],
            ig_out.at[:, pl.ds(start, n)],
            i_send.at[k, c], i_recv.at[k, c], fs_dev(d),
        )

    t_copies = [[token_copy(k, d, c) for k, d in enumerate(ORDER)] for c in range(len(T_CUTS))]
    i_copies = [[product_copy(k, d, c) for k, d in enumerate(ORDER)] for c in range(len(I_CUTS))]

    a_copies, b_copies, gb_copies, ga_copies = [], [], [], []
    for k in range(1, GA):
        rows = pl.ds(pl.multiple_of(a_peer(k) * RA, RA), RA)
        a_copies.append(remote(
            deq.at[rows], part_a.at[k - 1], a_send.at[k - 1], a_recv.at[k - 1], a_dev(k)
        ))
        ga_copies.append(remote(
            sum_a, full_a.at[a_id], ga_send.at[k - 1], ga_recv.at[k - 1], a_dev(k)
        ))
    for k in range(1, GB):
        b_copies.append(remote(
            mine_b.at[b_peer(k)], part_b.at[k - 1], b_send.at[k - 1], b_recv.at[k - 1], b_dev(k)
        ))
        gb_copies.append(remote(
            sum_b, full_b.at[b_id], gb_send.at[k - 1], gb_recv.at[k - 1], b_dev(k)
        ))

    r_copies = a_copies + b_copies + gb_copies + ga_copies

    def start(copies):
        for copy in copies:
            copy.start()

    def arrived(copies):
        for copy in copies:
            copy.wait_recv()

    def sent(copies):
        for copy in copies:
            copy.wait_send()

    def product(d, c):
        return lax.dot_general(
            cot[peer(d)], kp[pl.ds(c * WIDTH, WIDTH), :], (((1,), (1,)), ((), ())),
            preferred_element_type=jnp.float32,
        ).astype(jnp.bfloat16)

    def products(k):
        for c in range(CHUNKS):
            ig[k, :, pl.ds(c * WIDTH, WIDTH)] = product(ORDER[k], c)

    def own_product():
        for c in range(CHUNKS):
            first = pl.multiple_of(me * COLS + c * WIDTH, WIDTH)
            ig_out[:, pl.ds(first, WIDTH)] = product(0, c)

    def projection(c):
        arrived(t_copies[c])
        lo, n = T_CUTS[c]
        for at_col in range(lo, lo + n, WIDTH):
            cols = pl.ds(at_col, WIDTH)
            gp_out[cols, :] = lax.dot_general(
                tok[:, :, cols].reshape(NF * TOK, WIDTH), cot[...].reshape(NF * TOK, KV),
                (((0,), (0,)), ((), ())), preferred_element_type=jnp.float32,
            ).astype(jnp.bfloat16)

    def dequantize():
        loads[2].wait()
        loads[3].wait()
        spread = jnp.transpose(jnp.broadcast_to(scales[...], (BLOCK, ROWS)))
        deq[...] = codes[...].astype(jnp.float32) * spread
        start(a_copies)

    def sum_first():
        arrived(a_copies)
        total = deq[pl.ds(pl.multiple_of(a_id * RA, RA), RA)]
        for k in range(GA - 1):
            total = total + part_a[k]
        for b in range(GB):
            mine_b[b] = total[b * RB:(b + 1) * RB]
        start(b_copies)

    def sum_second():
        arrived(b_copies)
        total = mine_b[b_id]
        for k in range(GB - 1):
            total = total + part_b[k]
        sum_b[...] = total
        full_b[b_id] = total
        start(gb_copies)

    def gather_first():
        arrived(gb_copies)
        for b in range(GB):
            sum_a[b * RB:(b + 1) * RB] = full_b[b]
        full_a[a_id] = sum_a[...]
        start(ga_copies)

    def outer_step():
        loads[4].wait()
        loads[5].wait()
        arrived(ga_copies)
        delta = full_a[...].reshape(ROWS, BLOCK) / (GA * GB)
        moment_next = OUTER_MOMENTUM * moment[...] + delta
        np_out[...] = params[...] - OUTER_RATE * (delta + OUTER_MOMENTUM * moment_next)
        nm_out[...] = moment_next

    start(c_copies)
    start(t_copies[0])
    dequantize()
    arrived(c_copies)
    start(f_copies)
    start(t_copies[1])
    sum_first()
    loads[0].wait()
    loads[1].wait()
    products(1)
    products(2)
    sum_second()
    start(t_copies[2])
    gather_first()
    arrived(f_copies)
    products(0)
    own_product()
    start(t_copies[3])
    outer_step()
    start(i_copies[0])
    loads[6].wait()
    projection(0)
    projection(1)
    projection(2)
    projection(3)
    for row in i_copies:
        arrived(row)
    sent(c_copies + f_copies + r_copies)
    for row in t_copies:
        sent(row)
    for row in i_copies:
        sent(row)

def finish(*refs):
    n = len(refs) // 2
    sems = refs[-1]
    copies = [pltpu.make_async_copy(refs[k], refs[n + k], sems.at[k]) for k in range(n)]
    for copy in copies:
        copy.start()
    for copy in copies:
        copy.wait()


def local(tokens, key_proj, cotangent, codes, block_scales, outer_params, outer_moment):
    f32, bf16 = jnp.float32, jnp.bfloat16
    any_spec = pl.BlockSpec(memory_space=pl.ANY)
    hbm_spec = pl.BlockSpec(memory_space=pltpu.HBM)
    vmem_spec = pl.BlockSpec(memory_space=pltpu.VMEM)
    dma = pltpu.SemaphoreType.DMA
    vmem = pltpu.VMEM
    results = pl.pallas_call(
        kernel,
        out_shape=(
            pltpu.VMEM((COLS, KV), bf16),
            pltpu.VMEM((TOK, NF * COLS), bf16),
            pltpu.VMEM((ROWS, BLOCK), f32),
            pltpu.VMEM((ROWS, BLOCK), f32),
        ),
        in_specs=[hbm_spec] * 7,
        out_specs=(vmem_spec,) * 4,
        scratch_shapes=[
            vmem((NF, TOK, COLS), bf16),
            vmem((COLS, KV), bf16),
            vmem((NF, TOK, KV), bf16),
            vmem((NF - 1, TOK, COLS), bf16),
            vmem((ROWS, BLOCK), jnp.int32),
            vmem((1, ROWS), f32),
            vmem((ROWS, BLOCK), f32),
            vmem((ROWS, BLOCK), f32),
            vmem((ROWS, BLOCK), f32),
            vmem((GA - 1, RA, BLOCK), f32),
            vmem((GB, RB, BLOCK), f32),
            vmem((GB - 1, RB, BLOCK), f32),
            vmem((RB, BLOCK), f32),
            vmem((GB, RB, BLOCK), f32),
            vmem((RA, BLOCK), f32),
            vmem((GA, RA, BLOCK), f32),
            dma((7,)),
            dma((2,)), dma((2,)), dma((2,)), dma((2,)),
            dma((3, len(T_CUTS))), dma((3, len(T_CUTS))),
            dma((3, len(I_CUTS))), dma((3, len(I_CUTS))),
            dma((GA - 1,)), dma((GA - 1,)), dma((GB - 1,)), dma((GB - 1,)),
            dma((GB - 1,)), dma((GB - 1,)), dma((GA - 1,)), dma((GA - 1,)),
        ],
        compiler_params=pltpu.CompilerParams(
            collective_id=0, has_side_effects=True, vmem_limit_bytes=48 * 1024 * 1024
        ),
        name="step",
    )(
        tokens[0], key_proj[0], cotangent[0], codes.reshape(ROWS, BLOCK), block_scales,
        outer_params.reshape(ROWS, BLOCK), outer_moment.reshape(ROWS, BLOCK),
    )
    grad_proj, input_grad, new_params, new_moment = pl.pallas_call(
        finish,
        out_shape=tuple(pltpu.HBM(r.shape, r.dtype) for r in results),
        in_specs=[any_spec] * 4,
        out_specs=(hbm_spec,) * 4,
        scratch_shapes=[dma((4,))],
        compiler_params=pltpu.CompilerParams(vmem_limit_bytes=8 * 1024 * 1024),
        name="finish",
    )(*results)
    return grad_proj[None], input_grad[None], new_params.reshape(-1), new_moment.reshape(-1)


def solution(mesh):
    return jax.shard_map(
        local,
        mesh=mesh,
        in_specs=(
            P("rep", "fsdp", None),
            P("rep", "fsdp", None),
            P("rep", "fsdp", None),
            P("rep", "fsdp"),
            P("rep", "fsdp"),
            P("fsdp"),
            P("fsdp"),
        ),
        out_specs=(P("rep", "fsdp", None), P("rep", "fsdp", None), P("fsdp"), P("fsdp")),
        check_vma=False,
    )
```

```python
import functools

import jax
import jax.numpy as jnp
from jax import lax
from jax.experimental import pallas as pl
from jax.experimental.pallas import tpu as pltpu
from jax.sharding import PartitionSpec as P

BLOCK = 128
TOK = 240
KV = 512
COLS = 2048
NF = 4
OUTER_RATE = 0.7
OUTER_MOMENTUM = 0.9

WIDTH = 256
CHUNKS = COLS // WIDTH
T_CUTS = ((0, 512), (512, 512), (1024, 1024))
I_CUTS = ((0, 2048),)
UPPER = 128
ROWS = 256
GA = 8
GB = 8
RA = ROWS // GA
RB = RA // GB

ORDER = (2, 1, 3)

MESH = pl.DeviceIdType.MESH


def kernel(
    tok_hbm, kp_hbm, cot_hbm, codes_hbm, scales_hbm, params_hbm, moment_hbm,
    gp_out, ig_out, np_out, nm_out,
    tok, kp, cot, ig, codes, scales, params, moment,
    deq, part_a, mine_b, part_b, sum_b, full_b, sum_a, full_a,
    load_sem,
    c_send, c_recv, f_send, f_recv,
    t_send, t_recv, i_send, i_recv,
    a_send, a_recv, b_send, b_recv, gb_send, gb_recv, ga_send, ga_recv,
):
    rep = lax.axis_index("rep")
    me = lax.axis_index("fsdp")
    a_id = lax.rem(rep, GA)
    b_id = lax.div(rep, GA)

    def peer(d):
        return lax.rem(me + d, NF)

    def fs_dev(d):
        return (rep, peer(d))

    def a_peer(k):
        return lax.rem(a_id + k, GA)

    def b_peer(k):
        return lax.rem(b_id + k, GB)

    def a_dev(k):
        return (b_id * GA + a_peer(k), me)

    def b_dev(k):
        return (b_peer(k) * GA + a_id, me)

    def remote(src, dst, send, recv, dev):
        return pltpu.make_async_remote_copy(
            src_ref=src, dst_ref=dst, send_sem=send, recv_sem=recv,
            device_id=dev, device_id_type=MESH,
        )

    barrier = pltpu.get_barrier_semaphore()
    devs = [fs_dev(d) for d in ORDER]
    devs += [b_dev(k) for k in range(1, GB)] + [a_dev(k) for k in range(1, GA)]
    for dev in devs:
        pl.semaphore_signal(barrier, inc=1, device_id=dev, device_id_type=MESH)

    loads = [
        pltpu.make_async_copy(cot_hbm, cot.at[me], load_sem.at[0]),
        pltpu.make_async_copy(kp_hbm, kp, load_sem.at[1]),
        pltpu.make_async_copy(codes_hbm, codes, load_sem.at[2]),
        pltpu.make_async_copy(scales_hbm, scales, load_sem.at[3]),
        pltpu.make_async_copy(params_hbm, params, load_sem.at[4]),
        pltpu.make_async_copy(moment_hbm, moment, load_sem.at[5]),
        pltpu.make_async_copy(
            tok_hbm.at[:, pl.ds(pl.multiple_of(me * COLS, COLS), COLS)], tok.at[me], load_sem.at[6]
        ),
    ]
    for load in loads:
        load.start()

    pl.semaphore_wait(barrier, len(devs))

    c_copies = [
        remote(cot_hbm, cot.at[me], c_send.at[k], c_recv.at[k], fs_dev(d))
        for k, d in enumerate((1, 3))
    ]

    f_copies = []
    for k, (origin, target, lo, n) in enumerate(((3, 1, 0, UPPER), (1, 3, UPPER, TOK - UPPER))):
        part = cot.at[peer(origin), pl.ds(lo, n)]
        f_copies.append(remote(part, part, f_send.at[k], f_recv.at[k], fs_dev(target)))

    def token_copy(k, d, c):
        lo, n = T_CUTS[c]
        start = pl.multiple_of(peer(d) * COLS + lo, WIDTH)
        return remote(
            tok_hbm.at[:, pl.ds(start, n)],
            tok.at[me, :, pl.ds(lo, n)],
            t_send.at[k, c], t_recv.at[k, c], fs_dev(d),
        )

    def product_copy(k, d, c):
        lo, n = I_CUTS[c]
        start = pl.multiple_of(me * COLS + lo, WIDTH)
        return remote(
            ig.at[k, :, pl.ds(lo, n)],
            ig_out.at[:, pl.ds(start, n)],
            i_send.at[k, c], i_recv.at[k, c], fs_dev(d),
        )

    t_copies = [[token_copy(k, d, c) for k, d in enumerate(ORDER)] for c in range(len(T_CUTS))]
    i_copies = [[product_copy(k, d, c) for k, d in enumerate(ORDER)] for c in range(len(I_CUTS))]

    a_copies, b_copies, gb_copies, ga_copies = [], [], [], []
    for k in range(1, GA):
        rows = pl.ds(pl.multiple_of(a_peer(k) * RA, RA), RA)
        a_copies.append(remote(
            deq.at[rows], part_a.at[k - 1], a_send.at[k - 1], a_recv.at[k - 1], a_dev(k)
        ))
        ga_copies.append(remote(
            sum_a, full_a.at[a_id], ga_send.at[k - 1], ga_recv.at[k - 1], a_dev(k)
        ))
    for k in range(1, GB):
        b_copies.append(remote(
            mine_b.at[b_peer(k)], part_b.at[k - 1], b_send.at[k - 1], b_recv.at[k - 1], b_dev(k)
        ))
        gb_copies.append(remote(
            sum_b, full_b.at[b_id], gb_send.at[k - 1], gb_recv.at[k - 1], b_dev(k)
        ))

    r_copies = a_copies + b_copies + gb_copies + ga_copies

    def start(copies):
        for copy in copies:
            copy.start()

    def arrived(copies):
        for copy in copies:
            copy.wait_recv()

    def sent(copies):
        for copy in copies:
            copy.wait_send()

    def product(d, c):
        return lax.dot_general(
            cot[peer(d)], kp[pl.ds(c * WIDTH, WIDTH), :], (((1,), (1,)), ((), ())),
            preferred_element_type=jnp.float32,
        ).astype(jnp.bfloat16)

    def products(k):
        for c in range(CHUNKS):
            ig[k, :, pl.ds(c * WIDTH, WIDTH)] = product(ORDER[k], c)

    def own_product():
        for c in range(CHUNKS):
            first = pl.multiple_of(me * COLS + c * WIDTH, WIDTH)
            ig_out[:, pl.ds(first, WIDTH)] = product(0, c)

    def projection(c):
        arrived(t_copies[c])
        lo, n = T_CUTS[c]
        for at_col in range(lo, lo + n, WIDTH):
            cols = pl.ds(at_col, WIDTH)
            gp_out[cols, :] = lax.dot_general(
                tok[:, :, cols].reshape(NF * TOK, WIDTH), cot[...].reshape(NF * TOK, KV),
                (((0,), (0,)), ((), ())), preferred_element_type=jnp.float32,
            ).astype(jnp.bfloat16)

    def dequantize():
        loads[2].wait()
        loads[3].wait()
        spread = jnp.transpose(jnp.broadcast_to(scales[...], (BLOCK, ROWS)))
        deq[...] = codes[...].astype(jnp.float32) * spread
        start(a_copies)

    def sum_first():
        arrived(a_copies)
        total = deq[pl.ds(pl.multiple_of(a_id * RA, RA), RA)]
        for k in range(GA - 1):
            total = total + part_a[k]
        for b in range(GB):
            mine_b[b] = total[b * RB:(b + 1) * RB]
        start(b_copies)

    def sum_second():
        arrived(b_copies)
        total = mine_b[b_id]
        for k in range(GB - 1):
            total = total + part_b[k]
        sum_b[...] = total
        full_b[b_id] = total
        start(gb_copies)

    def gather_first():
        arrived(gb_copies)
        for b in range(GB):
            sum_a[b * RB:(b + 1) * RB] = full_b[b]
        full_a[a_id] = sum_a[...]
        start(ga_copies)

    def outer_step():
        loads[4].wait()
        loads[5].wait()
        arrived(ga_copies)
        delta = full_a[...].reshape(ROWS, BLOCK) / (GA * GB)
        moment_next = OUTER_MOMENTUM * moment[...] + delta
        np_out[...] = params[...] - OUTER_RATE * (delta + OUTER_MOMENTUM * moment_next)
        nm_out[...] = moment_next

    start(c_copies)
    start(t_copies[0])
    dequantize()
    arrived(c_copies)
    start(f_copies)
    start(t_copies[1])
    loads[0].wait()
    loads[1].wait()
    products(1)
    products(2)
    sum_first()
    arrived(f_copies)
    products(0)
    start(t_copies[2])
    sum_second()
    start(i_copies[0])
    own_product()
    gather_first()
    outer_step()
    loads[6].wait()
    projection(0)
    projection(1)
    projection(2)
    for row in i_copies:
        arrived(row)
    sent(c_copies + f_copies + r_copies)
    for row in t_copies:
        sent(row)
    for row in i_copies:
        sent(row)

def finish(*refs):
    n = len(refs) // 2
    sems = refs[-1]
    copies = [pltpu.make_async_copy(refs[k], refs[n + k], sems.at[k]) for k in range(n)]
    for copy in copies:
        copy.start()
    for copy in copies:
        copy.wait()


def local(tokens, key_proj, cotangent, codes, block_scales, outer_params, outer_moment):
    f32, bf16 = jnp.float32, jnp.bfloat16
    any_spec = pl.BlockSpec(memory_space=pl.ANY)
    hbm_spec = pl.BlockSpec(memory_space=pltpu.HBM)
    vmem_spec = pl.BlockSpec(memory_space=pltpu.VMEM)
    dma = pltpu.SemaphoreType.DMA
    vmem = pltpu.VMEM
    results = pl.pallas_call(
        kernel,
        out_shape=(
            pltpu.VMEM((COLS, KV), bf16),
            pltpu.VMEM((TOK, NF * COLS), bf16),
            pltpu.VMEM((ROWS, BLOCK), f32),
            pltpu.VMEM((ROWS, BLOCK), f32),
        ),
        in_specs=[hbm_spec] * 7,
        out_specs=(vmem_spec,) * 4,
        scratch_shapes=[
            vmem((NF, TOK, COLS), bf16),
            vmem((COLS, KV), bf16),
            vmem((NF, TOK, KV), bf16),
            vmem((NF - 1, TOK, COLS), bf16),
            vmem((ROWS, BLOCK), jnp.int32),
            vmem((1, ROWS), f32),
            vmem((ROWS, BLOCK), f32),
            vmem((ROWS, BLOCK), f32),
            vmem((ROWS, BLOCK), f32),
            vmem((GA - 1, RA, BLOCK), f32),
            vmem((GB, RB, BLOCK), f32),
            vmem((GB - 1, RB, BLOCK), f32),
            vmem((RB, BLOCK), f32),
            vmem((GB, RB, BLOCK), f32),
            vmem((RA, BLOCK), f32),
            vmem((GA, RA, BLOCK), f32),
            dma((7,)),
            dma((2,)), dma((2,)), dma((2,)), dma((2,)),
            dma((3, len(T_CUTS))), dma((3, len(T_CUTS))),
            dma((3, len(I_CUTS))), dma((3, len(I_CUTS))),
            dma((GA - 1,)), dma((GA - 1,)), dma((GB - 1,)), dma((GB - 1,)),
            dma((GB - 1,)), dma((GB - 1,)), dma((GA - 1,)), dma((GA - 1,)),
        ],
        compiler_params=pltpu.CompilerParams(
            collective_id=0, has_side_effects=True, vmem_limit_bytes=48 * 1024 * 1024
        ),
        name="step",
    )(
        tokens[0], key_proj[0], cotangent[0], codes.reshape(ROWS, BLOCK), block_scales,
        outer_params.reshape(ROWS, BLOCK), outer_moment.reshape(ROWS, BLOCK),
    )
    grad_proj, input_grad, new_params, new_moment = pl.pallas_call(
        finish,
        out_shape=tuple(pltpu.HBM(r.shape, r.dtype) for r in results),
        in_specs=[any_spec] * 4,
        out_specs=(hbm_spec,) * 4,
        scratch_shapes=[dma((4,))],
        compiler_params=pltpu.CompilerParams(vmem_limit_bytes=8 * 1024 * 1024),
        name="finish",
    )(*results)
    return grad_proj[None], input_grad[None], new_params.reshape(-1), new_moment.reshape(-1)


def solution(mesh):
    return jax.shard_map(
        local,
        mesh=mesh,
        in_specs=(
            P("rep", "fsdp", None),
            P("rep", "fsdp", None),
            P("rep", "fsdp", None),
            P("rep", "fsdp"),
            P("rep", "fsdp"),
            P("fsdp"),
            P("fsdp"),
        ),
        out_specs=(P("rep", "fsdp", None), P("rep", "fsdp", None), P("fsdp"), P("fsdp")),
        check_vma=False,
    )
```

```python
import functools

import jax
import jax.numpy as jnp
from jax import lax
from jax.experimental import pallas as pl
from jax.experimental.pallas import tpu as pltpu
from jax.sharding import PartitionSpec as P

BLOCK = 128
TOK = 240
KV = 512
COLS = 2048
NF = 4
OUTER_RATE = 0.7
OUTER_MOMENTUM = 0.9

WIDTH = 256
CHUNKS = COLS // WIDTH
T_CUTS = ((0, 512), (512, 768), (1280, 768))
I_CUTS = ((0, 2048),)
UPPER = 128
ROWS = 256
GA = 8
GB = 8
RA = ROWS // GA
RB = RA // GB

ORDER = (2, 1, 3)

MESH = pl.DeviceIdType.MESH


def kernel(
    tok_hbm, kp_hbm, cot_hbm, codes_hbm, scales_hbm, params_hbm, moment_hbm,
    gp_out, ig_out, np_out, nm_out,
    tok, kp, cot, ig, codes, scales, params, moment,
    deq, part_a, mine_b, part_b, sum_b, full_b, sum_a, full_a,
    load_sem,
    c_send, c_recv, f_send, f_recv,
    t_send, t_recv, i_send, i_recv,
    a_send, a_recv, b_send, b_recv, gb_send, gb_recv, ga_send, ga_recv,
):
    rep = lax.axis_index("rep")
    me = lax.axis_index("fsdp")
    a_id = lax.rem(rep, GA)
    b_id = lax.div(rep, GA)

    def peer(d):
        return lax.rem(me + d, NF)

    def fs_dev(d):
        return (rep, peer(d))

    def a_peer(k):
        return lax.rem(a_id + k, GA)

    def b_peer(k):
        return lax.rem(b_id + k, GB)

    def a_dev(k):
        return (b_id * GA + a_peer(k), me)

    def b_dev(k):
        return (b_peer(k) * GA + a_id, me)

    def remote(src, dst, send, recv, dev):
        return pltpu.make_async_remote_copy(
            src_ref=src, dst_ref=dst, send_sem=send, recv_sem=recv,
            device_id=dev, device_id_type=MESH,
        )

    barrier = pltpu.get_barrier_semaphore()
    devs = [fs_dev(d) for d in ORDER]
    devs += [b_dev(k) for k in range(1, GB)] + [a_dev(k) for k in range(1, GA)]
    for dev in devs:
        pl.semaphore_signal(barrier, inc=1, device_id=dev, device_id_type=MESH)

    pl.semaphore_wait(barrier, len(devs))

    c_copies = [
        remote(cot_hbm, cot.at[me], c_send.at[k], c_recv.at[k], fs_dev(d))
        for k, d in enumerate((1, 3))
    ]

    f_copies = []
    for k, (origin, target, lo, n) in enumerate(((3, 1, 0, UPPER), (1, 3, UPPER, TOK - UPPER))):
        part = cot.at[peer(origin), pl.ds(lo, n)]
        f_copies.append(remote(part, part, f_send.at[k], f_recv.at[k], fs_dev(target)))

    def token_copy(k, d, c):
        lo, n = T_CUTS[c]
        start = pl.multiple_of(peer(d) * COLS + lo, WIDTH)
        return remote(
            tok_hbm.at[:, pl.ds(start, n)],
            tok.at[me, :, pl.ds(lo, n)],
            t_send.at[k, c], t_recv.at[k, c], fs_dev(d),
        )

    def product_copy(k, d, c):
        lo, n = I_CUTS[c]
        start = pl.multiple_of(me * COLS + lo, WIDTH)
        return remote(
            ig.at[k, :, pl.ds(lo, n)],
            ig_out.at[:, pl.ds(start, n)],
            i_send.at[k, c], i_recv.at[k, c], fs_dev(d),
        )

    t_copies = [[token_copy(k, d, c) for k, d in enumerate(ORDER)] for c in range(len(T_CUTS))]
    i_copies = [[product_copy(k, d, c) for k, d in enumerate(ORDER)] for c in range(len(I_CUTS))]

    a_copies, b_copies, gb_copies, ga_copies = [], [], [], []
    for k in range(1, GA):
        rows = pl.ds(pl.multiple_of(a_peer(k) * RA, RA), RA)
        a_copies.append(remote(
            deq.at[rows], part_a.at[k - 1], a_send.at[k - 1], a_recv.at[k - 1], a_dev(k)
        ))
        ga_copies.append(remote(
            sum_a, full_a.at[a_id], ga_send.at[k - 1], ga_recv.at[k - 1], a_dev(k)
        ))
    for k in range(1, GB):
        b_copies.append(remote(
            mine_b.at[b_peer(k)], part_b.at[k - 1], b_send.at[k - 1], b_recv.at[k - 1], b_dev(k)
        ))
        gb_copies.append(remote(
            sum_b, full_b.at[b_id], gb_send.at[k - 1], gb_recv.at[k - 1], b_dev(k)
        ))

    r_copies = a_copies + b_copies + gb_copies + ga_copies

    loads = [
        pltpu.make_async_copy(cot_hbm, cot.at[me], load_sem.at[0]),
        pltpu.make_async_copy(kp_hbm, kp, load_sem.at[1]),
        pltpu.make_async_copy(codes_hbm, codes, load_sem.at[2]),
        pltpu.make_async_copy(scales_hbm, scales, load_sem.at[3]),
        pltpu.make_async_copy(params_hbm, params, load_sem.at[4]),
        pltpu.make_async_copy(moment_hbm, moment, load_sem.at[5]),
        pltpu.make_async_copy(
            tok_hbm.at[:, pl.ds(pl.multiple_of(me * COLS, COLS), COLS)], tok.at[me], load_sem.at[6]
        ),
    ]

    def start(copies):
        for copy in copies:
            copy.start()

    def arrived(copies):
        for copy in copies:
            copy.wait_recv()

    def sent(copies):
        for copy in copies:
            copy.wait_send()

    def product(d, c):
        return lax.dot_general(
            cot[peer(d)], kp[pl.ds(c * WIDTH, WIDTH), :], (((1,), (1,)), ((), ())),
            preferred_element_type=jnp.float32,
        ).astype(jnp.bfloat16)

    def products(k):
        for c in range(CHUNKS):
            ig[k, :, pl.ds(c * WIDTH, WIDTH)] = product(ORDER[k], c)

    def own_product():
        for c in range(CHUNKS):
            first = pl.multiple_of(me * COLS + c * WIDTH, WIDTH)
            ig_out[:, pl.ds(first, WIDTH)] = product(0, c)

    def projection(c):
        arrived(t_copies[c])
        lo, n = T_CUTS[c]
        for at_col in range(lo, lo + n, WIDTH):
            cols = pl.ds(at_col, WIDTH)
            gp_out[cols, :] = lax.dot_general(
                tok[:, :, cols].reshape(NF * TOK, WIDTH), cot[...].reshape(NF * TOK, KV),
                (((0,), (0,)), ((), ())), preferred_element_type=jnp.float32,
            ).astype(jnp.bfloat16)

    def dequantize():
        loads[2].wait()
        loads[3].wait()
        spread = jnp.transpose(jnp.broadcast_to(scales[...], (BLOCK, ROWS)))
        deq[...] = codes[...].astype(jnp.float32) * spread
        start(a_copies)

    def sum_first():
        arrived(a_copies)
        total = deq[pl.ds(pl.multiple_of(a_id * RA, RA), RA)]
        for k in range(GA - 1):
            total = total + part_a[k]
        for b in range(GB):
            mine_b[b] = total[b * RB:(b + 1) * RB]
        start(b_copies)

    def sum_second():
        arrived(b_copies)
        total = mine_b[b_id]
        for k in range(GB - 1):
            total = total + part_b[k]
        sum_b[...] = total
        full_b[b_id] = total
        start(gb_copies)

    def gather_first():
        arrived(gb_copies)
        for b in range(GB):
            sum_a[b * RB:(b + 1) * RB] = full_b[b]
        full_a[a_id] = sum_a[...]
        start(ga_copies)

    def outer_step():
        loads[4].wait()
        loads[5].wait()
        arrived(ga_copies)
        delta = full_a[...].reshape(ROWS, BLOCK) / (GA * GB)
        moment_next = OUTER_MOMENTUM * moment[...] + delta
        np_out[...] = params[...] - OUTER_RATE * (delta + OUTER_MOMENTUM * moment_next)
        nm_out[...] = moment_next

    start(c_copies)
    start(t_copies[0])
    start(loads[2:4])
    start(loads[:2])
    start(loads[4:])
    dequantize()
    arrived(c_copies)
    start(f_copies)
    start(t_copies[1])
    loads[0].wait()
    loads[1].wait()
    products(1)
    products(2)
    sum_first()
    arrived(f_copies)
    products(0)
    start(t_copies[2])
    sum_second()
    start(i_copies[0])
    own_product()
    gather_first()
    outer_step()
    loads[6].wait()
    projection(0)
    projection(1)
    projection(2)
    sent(c_copies + f_copies + r_copies)
    for row in t_copies:
        sent(row)
    for row in i_copies:
        arrived(row)
    for row in i_copies:
        sent(row)

def finish(*refs):
    n = len(refs) // 2
    sems = refs[-1]
    copies = [pltpu.make_async_copy(refs[k], refs[n + k], sems.at[k]) for k in range(n)]
    for copy in copies:
        copy.start()
    for copy in copies:
        copy.wait()


def local(tokens, key_proj, cotangent, codes, block_scales, outer_params, outer_moment):
    f32, bf16 = jnp.float32, jnp.bfloat16
    any_spec = pl.BlockSpec(memory_space=pl.ANY)
    hbm_spec = pl.BlockSpec(memory_space=pltpu.HBM)
    vmem_spec = pl.BlockSpec(memory_space=pltpu.VMEM)
    dma = pltpu.SemaphoreType.DMA
    vmem = pltpu.VMEM
    results = pl.pallas_call(
        kernel,
        out_shape=(
            pltpu.VMEM((COLS, KV), bf16),
            pltpu.VMEM((TOK, NF * COLS), bf16),
            pltpu.VMEM((ROWS, BLOCK), f32),
            pltpu.VMEM((ROWS, BLOCK), f32),
        ),
        in_specs=[hbm_spec] * 7,
        out_specs=(vmem_spec,) * 4,
        scratch_shapes=[
            vmem((NF, TOK, COLS), bf16),
            vmem((COLS, KV), bf16),
            vmem((NF, TOK, KV), bf16),
            vmem((NF - 1, TOK, COLS), bf16),
            vmem((ROWS, BLOCK), jnp.int32),
            vmem((1, ROWS), f32),
            vmem((ROWS, BLOCK), f32),
            vmem((ROWS, BLOCK), f32),
            vmem((ROWS, BLOCK), f32),
            vmem((GA - 1, RA, BLOCK), f32),
            vmem((GB, RB, BLOCK), f32),
            vmem((GB - 1, RB, BLOCK), f32),
            vmem((RB, BLOCK), f32),
            vmem((GB, RB, BLOCK), f32),
            vmem((RA, BLOCK), f32),
            vmem((GA, RA, BLOCK), f32),
            dma((7,)),
            dma((2,)), dma((2,)), dma((2,)), dma((2,)),
            dma((3, len(T_CUTS))), dma((3, len(T_CUTS))),
            dma((3, len(I_CUTS))), dma((3, len(I_CUTS))),
            dma((GA - 1,)), dma((GA - 1,)), dma((GB - 1,)), dma((GB - 1,)),
            dma((GB - 1,)), dma((GB - 1,)), dma((GA - 1,)), dma((GA - 1,)),
        ],
        compiler_params=pltpu.CompilerParams(
            collective_id=0, has_side_effects=True, vmem_limit_bytes=48 * 1024 * 1024
        ),
        name="step",
    )(
        tokens[0], key_proj[0], cotangent[0], codes.reshape(ROWS, BLOCK), block_scales,
        outer_params.reshape(ROWS, BLOCK), outer_moment.reshape(ROWS, BLOCK),
    )
    grad_proj, input_grad, new_params, new_moment = pl.pallas_call(
        finish,
        out_shape=tuple(pltpu.HBM(r.shape, r.dtype) for r in results),
        in_specs=[any_spec] * 4,
        out_specs=(hbm_spec,) * 4,
        scratch_shapes=[dma((4,))],
        compiler_params=pltpu.CompilerParams(vmem_limit_bytes=8 * 1024 * 1024),
        name="finish",
    )(*results)
    return grad_proj[None], input_grad[None], new_params.reshape(-1), new_moment.reshape(-1)


def solution(mesh):
    return jax.shard_map(
        local,
        mesh=mesh,
        in_specs=(
            P("rep", "fsdp", None),
            P("rep", "fsdp", None),
            P("rep", "fsdp", None),
            P("rep", "fsdp"),
            P("rep", "fsdp"),
            P("fsdp"),
            P("fsdp"),
        ),
        out_specs=(P("rep", "fsdp", None), P("rep", "fsdp", None), P("fsdp"), P("fsdp")),
        check_vma=False,
    )
```

```python
import functools

import jax
import jax.numpy as jnp
from jax import lax
from jax.experimental import pallas as pl
from jax.experimental.pallas import tpu as pltpu
from jax.sharding import PartitionSpec as P

BLOCK = 128
TOK = 240
KV = 512
COLS = 2048
NF = 4
OUTER_RATE = 0.7
OUTER_MOMENTUM = 0.9

WIDTH = 256
CHUNKS = COLS // WIDTH
T_CUTS = ((0, 512), (512, 768), (1280, 768))
I_CUTS = ((0, 2048),)
UPPER = 128
ROWS = 256
GA = 8
GB = 8
RA = ROWS // GA
RB = RA // GB

ORDER = (2, 1, 3)

MESH = pl.DeviceIdType.MESH


def kernel(
    tok_hbm, kp_hbm, cot_hbm, codes_hbm, scales_hbm, params_hbm, moment_hbm,
    gp_out, ig_out, np_out, nm_out,
    tok, kp, cot, ig, codes, scales, params, moment,
    deq, part_a, mine_b, part_b, sum_b, full_b, sum_a, full_a,
    load_sem,
    c_send, c_recv, f_send, f_recv,
    t_send, t_recv, i_send, i_recv,
    a_send, a_recv, b_send, b_recv, gb_send, gb_recv, ga_send, ga_recv,
):
    rep = lax.axis_index("rep")
    me = lax.axis_index("fsdp")
    a_id = lax.rem(rep, GA)
    b_id = lax.div(rep, GA)

    def peer(d):
        return lax.rem(me + d, NF)

    def fs_dev(d):
        return (rep, peer(d))

    def a_peer(k):
        return lax.rem(a_id + k, GA)

    def b_peer(k):
        return lax.rem(b_id + k, GB)

    def a_dev(k):
        return (b_id * GA + a_peer(k), me)

    def b_dev(k):
        return (b_peer(k) * GA + a_id, me)

    def remote(src, dst, send, recv, dev):
        return pltpu.make_async_remote_copy(
            src_ref=src, dst_ref=dst, send_sem=send, recv_sem=recv,
            device_id=dev, device_id_type=MESH,
        )

    barrier = pltpu.get_barrier_semaphore()
    devs = [fs_dev(d) for d in ORDER]
    devs += [b_dev(k) for k in range(1, GB)] + [a_dev(k) for k in range(1, GA)]
    for dev in devs:
        pl.semaphore_signal(barrier, inc=1, device_id=dev, device_id_type=MESH)

    pl.semaphore_wait(barrier, len(devs))

    c_copies = [
        remote(cot_hbm, cot.at[me], c_send.at[k], c_recv.at[k], fs_dev(d))
        for k, d in enumerate((1, 3))
    ]

    f_copies = []
    for k, (origin, target, lo, n) in enumerate(((3, 1, 0, UPPER), (1, 3, UPPER, TOK - UPPER))):
        part = cot.at[peer(origin), pl.ds(lo, n)]
        f_copies.append(remote(part, part, f_send.at[k], f_recv.at[k], fs_dev(target)))

    def token_copy(k, d, c):
        lo, n = T_CUTS[c]
        start = pl.multiple_of(peer(d) * COLS + lo, WIDTH)
        return remote(
            tok_hbm.at[:, pl.ds(start, n)],
            tok.at[me, :, pl.ds(lo, n)],
            t_send.at[k, c], t_recv.at[k, c], fs_dev(d),
        )

    def product_copy(k, d, c):
        lo, n = I_CUTS[c]
        start = pl.multiple_of(me * COLS + lo, WIDTH)
        return remote(
            ig.at[k, :, pl.ds(lo, n)],
            ig_out.at[:, pl.ds(start, n)],
            i_send.at[k, c], i_recv.at[k, c], fs_dev(d),
        )

    t_copies = [[token_copy(k, d, c) for k, d in enumerate(ORDER)] for c in range(len(T_CUTS))]
    i_copies = [[product_copy(k, d, c) for k, d in enumerate(ORDER)] for c in range(len(I_CUTS))]

    a_copies, b_copies, gb_copies, ga_copies = [], [], [], []
    for k in range(1, GA):
        rows = pl.ds(pl.multiple_of(a_peer(k) * RA, RA), RA)
        a_copies.append(remote(
            deq.at[rows], part_a.at[k - 1], a_send.at[k - 1], a_recv.at[k - 1], a_dev(k)
        ))
        ga_copies.append(remote(
            sum_a, full_a.at[a_id], ga_send.at[k - 1], ga_recv.at[k - 1], a_dev(k)
        ))
    for k in range(1, GB):
        b_copies.append(remote(
            mine_b.at[b_peer(k)], part_b.at[k - 1], b_send.at[k - 1], b_recv.at[k - 1], b_dev(k)
        ))
        gb_copies.append(remote(
            sum_b, full_b.at[b_id], gb_send.at[k - 1], gb_recv.at[k - 1], b_dev(k)
        ))

    r_copies = a_copies + b_copies + gb_copies + ga_copies

    loads = [
        pltpu.make_async_copy(cot_hbm, cot.at[me], load_sem.at[0]),
        pltpu.make_async_copy(kp_hbm, kp, load_sem.at[1]),
        pltpu.make_async_copy(codes_hbm, codes, load_sem.at[2]),
        pltpu.make_async_copy(scales_hbm, scales, load_sem.at[3]),
        pltpu.make_async_copy(params_hbm, params, load_sem.at[4]),
        pltpu.make_async_copy(moment_hbm, moment, load_sem.at[5]),
        pltpu.make_async_copy(
            tok_hbm.at[:, pl.ds(pl.multiple_of(me * COLS, COLS), COLS)], tok.at[me], load_sem.at[6]
        ),
    ]

    def start(copies):
        for copy in copies:
            copy.start()

    def arrived(copies):
        for copy in copies:
            copy.wait_recv()

    def sent(copies):
        for copy in copies:
            copy.wait_send()

    def product(d, c):
        return lax.dot_general(
            cot[peer(d)], kp[pl.ds(c * WIDTH, WIDTH), :], (((1,), (1,)), ((), ())),
            preferred_element_type=jnp.float32,
        ).astype(jnp.bfloat16)

    def products(k):
        for c in range(CHUNKS):
            ig[k, :, pl.ds(c * WIDTH, WIDTH)] = product(ORDER[k], c)

    def own_product():
        for c in range(CHUNKS):
            first = pl.multiple_of(me * COLS + c * WIDTH, WIDTH)
            ig_out[:, pl.ds(first, WIDTH)] = product(0, c)

    def projection(c):
        arrived(t_copies[c])
        lo, n = T_CUTS[c]
        for at_col in range(lo, lo + n, WIDTH):
            cols = pl.ds(at_col, WIDTH)
            gp_out[cols, :] = lax.dot_general(
                tok[:, :, cols].reshape(NF * TOK, WIDTH), cot[...].reshape(NF * TOK, KV),
                (((0,), (0,)), ((), ())), preferred_element_type=jnp.float32,
            ).astype(jnp.bfloat16)

    def dequantize():
        loads[2].wait()
        loads[3].wait()
        spread = jnp.transpose(jnp.broadcast_to(scales[...], (BLOCK, ROWS)))
        deq[...] = codes[...].astype(jnp.float32) * spread
        start(a_copies)

    def sum_first():
        arrived(a_copies)
        total = deq[pl.ds(pl.multiple_of(a_id * RA, RA), RA)]
        for k in range(GA - 1):
            total = total + part_a[k]
        for b in range(GB):
            mine_b[b] = total[b * RB:(b + 1) * RB]
        start(b_copies)

    def sum_second():
        arrived(b_copies)
        total = mine_b[b_id]
        for k in range(GB - 1):
            total = total + part_b[k]
        sum_b[...] = total
        full_b[b_id] = total
        start(gb_copies)

    def gather_first():
        arrived(gb_copies)
        for b in range(GB):
            sum_a[b * RB:(b + 1) * RB] = full_b[b]
        full_a[a_id] = sum_a[...]
        start(ga_copies)

    def outer_step():
        loads[4].wait()
        loads[5].wait()
        arrived(ga_copies)
        delta = full_a[...].reshape(ROWS, BLOCK) / (GA * GB)
        moment_next = OUTER_MOMENTUM * moment[...] + delta
        np_out[...] = params[...] - OUTER_RATE * (delta + OUTER_MOMENTUM * moment_next)
        nm_out[...] = moment_next

    start(c_copies)
    start(t_copies[0])
    start(loads[2:4])
    start(loads[:2])
    start(loads[4:])
    arrived(c_copies)
    start(f_copies)
    dequantize()
    start(t_copies[1])
    loads[0].wait()
    loads[1].wait()
    products(1)
    products(2)
    sum_first()
    arrived(f_copies)
    products(0)
    start(t_copies[2])
    sum_second()
    start(i_copies[0])
    own_product()
    gather_first()
    outer_step()
    loads[6].wait()
    projection(0)
    projection(1)
    projection(2)
    sent(c_copies + f_copies + r_copies)
    for row in t_copies:
        sent(row)
    for row in i_copies:
        arrived(row)
    for row in i_copies:
        sent(row)

def finish(*refs):
    n = len(refs) // 2
    sems = refs[-1]
    copies = [pltpu.make_async_copy(refs[k], refs[n + k], sems.at[k]) for k in range(n)]
    for copy in copies:
        copy.start()
    for copy in copies:
        copy.wait()


def local(tokens, key_proj, cotangent, codes, block_scales, outer_params, outer_moment):
    f32, bf16 = jnp.float32, jnp.bfloat16
    any_spec = pl.BlockSpec(memory_space=pl.ANY)
    hbm_spec = pl.BlockSpec(memory_space=pltpu.HBM)
    vmem_spec = pl.BlockSpec(memory_space=pltpu.VMEM)
    dma = pltpu.SemaphoreType.DMA
    vmem = pltpu.VMEM
    results = pl.pallas_call(
        kernel,
        out_shape=(
            pltpu.VMEM((COLS, KV), bf16),
            pltpu.VMEM((TOK, NF * COLS), bf16),
            pltpu.VMEM((ROWS, BLOCK), f32),
            pltpu.VMEM((ROWS, BLOCK), f32),
        ),
        in_specs=[hbm_spec] * 7,
        out_specs=(vmem_spec,) * 4,
        scratch_shapes=[
            vmem((NF, TOK, COLS), bf16),
            vmem((COLS, KV), bf16),
            vmem((NF, TOK, KV), bf16),
            vmem((NF - 1, TOK, COLS), bf16),
            vmem((ROWS, BLOCK), jnp.int32),
            vmem((1, ROWS), f32),
            vmem((ROWS, BLOCK), f32),
            vmem((ROWS, BLOCK), f32),
            vmem((ROWS, BLOCK), f32),
            vmem((GA - 1, RA, BLOCK), f32),
            vmem((GB, RB, BLOCK), f32),
            vmem((GB - 1, RB, BLOCK), f32),
            vmem((RB, BLOCK), f32),
            vmem((GB, RB, BLOCK), f32),
            vmem((RA, BLOCK), f32),
            vmem((GA, RA, BLOCK), f32),
            dma((7,)),
            dma((2,)), dma((2,)), dma((2,)), dma((2,)),
            dma((3, len(T_CUTS))), dma((3, len(T_CUTS))),
            dma((3, len(I_CUTS))), dma((3, len(I_CUTS))),
            dma((GA - 1,)), dma((GA - 1,)), dma((GB - 1,)), dma((GB - 1,)),
            dma((GB - 1,)), dma((GB - 1,)), dma((GA - 1,)), dma((GA - 1,)),
        ],
        compiler_params=pltpu.CompilerParams(
            collective_id=0, has_side_effects=True, vmem_limit_bytes=48 * 1024 * 1024
        ),
        name="step",
    )(
        tokens[0], key_proj[0], cotangent[0], codes.reshape(ROWS, BLOCK), block_scales,
        outer_params.reshape(ROWS, BLOCK), outer_moment.reshape(ROWS, BLOCK),
    )
    grad_proj, input_grad, new_params, new_moment = pl.pallas_call(
        finish,
        out_shape=tuple(pltpu.HBM(r.shape, r.dtype) for r in results),
        in_specs=[any_spec] * 4,
        out_specs=(hbm_spec,) * 4,
        scratch_shapes=[dma((4,))],
        compiler_params=pltpu.CompilerParams(vmem_limit_bytes=8 * 1024 * 1024),
        name="finish",
    )(*results)
    return grad_proj[None], input_grad[None], new_params.reshape(-1), new_moment.reshape(-1)


def solution(mesh):
    return jax.shard_map(
        local,
        mesh=mesh,
        in_specs=(
            P("rep", "fsdp", None),
            P("rep", "fsdp", None),
            P("rep", "fsdp", None),
            P("rep", "fsdp"),
            P("rep", "fsdp"),
            P("fsdp"),
            P("fsdp"),
        ),
        out_specs=(P("rep", "fsdp", None), P("rep", "fsdp", None), P("fsdp"), P("fsdp")),
        check_vma=False,
    )
```
